32 devices in a mesh: tilt: 4 (over z), pos: 8 (over y, x, core).
Axes of the slice: x: 2, y: 2, z: 4, core: 2. Of those that a mesh axis runs over, the one named last changes fastest.
Arguments:
- intensity: bfloat16 [4, 128, 256, 256], P('tilt', 'pos'), may hold values from 0 to 1
- positions: int32 [4, 128, 2], P('tilt', 'pos'), may hold values from 0 to 512, as said below
- counts: int32 [4, 8], P('tilt', 'pos'), may hold values from 8 to 16, as said below
- object_field: bfloat16 [4, 2, 768, 768], P('tilt', None, 'pos'), may hold values from 0.5 to 1.5
- probe: float32 [2, 256, 256], replicated, may hold values from -3 to 3
Outputs:
- object_grad: float32 [4, 2, 768, 768], P('tilt', None, 'pos')
- probe_grad: float32 [2, 256, 256], replicated
The draws below stay inside these ranges and needn't reach their ends.
Inputs may be any that keep to these rules, and one draw needn't show every extreme that they name: The batch pairs each flat tilt t < 2 with the steep tilt t + 2: for every position index p, counts[t, p] + counts[t + 2, p] = 24 and counts[t, p] <= 12. `positions`: the row offset of a slot of position index p lies between max(0, (p - 2) * 96) and min(512, (p + 256 // 96 + 1) * 96 - 256); column offsets lie between 0 and 512.
All inputs are finite; a program needn't handle non-finite values.
Results may differ from the reference program's by a relative error of at most 0.0017.
The reference program's roundings to bfloat16 on the way count: a program that leaves them out, or rounds other values in their place, can miss the bound.
Values may be sent and summed in bfloat16 or wider, within the bound.
A program may use at most 128 MiB of HBM per device.

```python
import math
import jax
import jax.numpy as jnp
from jax import lax

W = 256
FMAX = 16
CMIN = 8
OBJ_DEV = 96
TILTS = 4
OBJ = 768
SLOTS = 128
N_POS = 8


def draw_counts(key, part):
    paired = TILTS // 2
    offset = jax.random.randint(jax.random.fold_in(key, 17), (paired, N_POS), 0, 3).astype(jnp.int32)
    offset = offset.at[0].set(0)
    flat = CMIN + offset
    steep = FMAX - offset
    return jnp.concatenate([flat, steep], 0).astype(jnp.int32)


def draw_positions(key, part):
    slot = jnp.arange(SLOTS, dtype=jnp.int32)
    owner = slot // FMAX
    reach = W // OBJ_DEV
    lowest = jnp.maximum((owner - reach) * OBJ_DEV, 0)
    highest = jnp.minimum((owner + reach + 1) * OBJ_DEV - W, OBJ - W)
    rows = jax.random.randint(jax.random.fold_in(key, 3), (TILTS, SLOTS), lowest[None, :], highest[None, :] + 1).astype(jnp.int32)
    columns = jax.random.randint(jax.random.fold_in(key, 5), (TILTS, SLOTS), 0, OBJ - W + 1).astype(jnp.int32)
    rows = rows.at[:, 0].set(0)
    rows = rows.at[:, SLOTS - 1].set(OBJ - W)
    columns = columns.at[:, 0].set(0)
    columns = columns.at[:, SLOTS - 1].set(OBJ - W)
    return jnp.stack([rows, columns], -1).astype(jnp.int32)


def shard_levels(own_key, dims, split, low, top_value):
    gain, own = 1.0, jax.random.fold_in(own_key, 6)
    for axis_at, parts in split:
        steps = jnp.exp(jax.random.uniform(jax.random.fold_in(own, axis_at), (parts,), jnp.float32, low / len(split), top_value / len(split)))
        gain = gain * jnp.repeat(steps, dims[axis_at] // parts).reshape([-1 if axis == axis_at else 1 for axis in range(len(dims))])
    return gain


def noise(stream_key, shape, deviation, bound, kind=jnp.bfloat16):
    array = deviation * jax.random.normal(stream_key, shape, jnp.float32)
    return jnp.clip(array, min=-bound, max=bound).astype(kind)


def setup_inputs(seed: int = 0) -> dict:
    seeds = jax.random.split(jax.random.key(seed), 6)
    intensity = jnp.clip(1.0 * jax.random.uniform(seeds[0], (TILTS, SLOTS, W, W), jnp.float32) ** shard_levels(seeds[0], (TILTS, SLOTS, W, W), ((0, 4), (1, 8)), -0.2, 0.2), 0.0, 1.0).astype(jnp.bfloat16)
    positions = draw_positions(jax.random.fold_in(seeds[5], 71), 0)
    counts = draw_counts(jax.random.fold_in(seeds[5], 71), 0)
    object_field = jnp.clip(0.5 + 1.0 * jax.random.uniform(seeds[3], (TILTS, 2, OBJ, OBJ), jnp.float32) ** shard_levels(seeds[3], (TILTS, 2, OBJ, OBJ), ((0, 4), (2, 8)), -0.2, 0.2), 0.5, 1.5).astype(jnp.bfloat16)
    probe = noise(seeds[4], (2, W, W), 0.5, 3.0, jnp.float32)
    return dict(intensity=intensity, positions=positions, counts=counts, object_field=object_field, probe=probe)


def dft_tables(length):
    index = jnp.arange(length, dtype=jnp.int32)
    phase = (index[:, None] * index[None, :] % length).astype(jnp.float32) * (2.0 * math.pi / length)
    cosine = jnp.cos(phase) / math.sqrt(length)
    sine = jnp.sin(phase) / math.sqrt(length)
    forward_table = jnp.stack([jnp.stack([cosine, -sine]), jnp.stack([sine, cosine])]).astype(jnp.bfloat16)
    inverse_table = jnp.stack([jnp.stack([cosine, sine]), jnp.stack([-sine, cosine])]).astype(jnp.bfloat16)
    return (forward_table, inverse_table)

def widen(field):
    return lax.optimization_barrier(field).astype(jnp.float32)

def along_columns(field, table):
    return jnp.einsum('fcry,cdyk->fdrk', widen(field), widen(table))

def along_rows(field, table):
    return jnp.einsum('fcyk,cdyr->fdrk', widen(field), widen(table))

def frame_grads(frames, patches, probe, forward_table, inverse_table, live):
    probe_re, probe_im = (probe[0], probe[1])
    patch_re = patches[:, 0].astype(jnp.float32)
    patch_im = patches[:, 1].astype(jnp.float32)
    exit_wave = jnp.stack([probe_re * patch_re - probe_im * patch_im, probe_re * patch_im + probe_im * patch_re], 1).astype(jnp.bfloat16)
    half = along_columns(exit_wave, forward_table).astype(jnp.bfloat16)
    far = along_rows(half, forward_table)
    misfit = far[:, 0] * far[:, 0] + far[:, 1] * far[:, 1] - frames.astype(jnp.float32)
    back = (far * misfit[:, None]).astype(jnp.bfloat16)
    middle = along_rows(back, inverse_table).astype(jnp.bfloat16)
    wave = along_columns(middle, inverse_table)
    wave_re, wave_im = (wave[:, 0], wave[:, 1])
    grads = jnp.stack([probe_re * wave_re + probe_im * wave_im, probe_re * wave_im - probe_im * wave_re], 1).astype(jnp.bfloat16)
    grads = jnp.where(live[:, None, None, None], grads, jnp.zeros_like(grads))
    weight = live.astype(jnp.float32)[:, None, None]
    numer_re = lax.optimization_barrier(jnp.sum((patch_re * wave_re + patch_im * wave_im) * weight, axis=0))
    numer_im = lax.optimization_barrier(jnp.sum((patch_re * wave_im - patch_im * wave_re) * weight, axis=0))
    denom = lax.optimization_barrier(jnp.sum((patch_re * patch_re + patch_im * patch_im) * weight, axis=0))
    return (grads, jnp.stack([numer_re, numer_im]), denom)

def place_patches(total, pieces, places):
    zero = jnp.zeros((), jnp.int32)

    def add_one(index, total):
        start = (zero, places[index, 0].astype(jnp.int32), places[index, 1].astype(jnp.int32))
        current = lax.dynamic_slice(total, start, (2, W, W))
        return lax.dynamic_update_slice(total, current + pieces[index].astype(jnp.float32), start)
    return lax.fori_loop(0, pieces.shape[0], add_one, total)

def reference(intensity, positions, counts, object_field, probe):
    forward_table, inverse_table = dft_tables(W)
    lane = jnp.arange(FMAX, dtype=jnp.int32)
    zero = jnp.zeros((), jnp.int32)

    def one_tilt(carry, inputs):
        numer, denom = carry
        frames, places, column, image = inputs

        def cut(place):
            return lax.dynamic_slice(image, (zero, place[0].astype(jnp.int32), place[1].astype(jnp.int32)), (2, W, W))

        def one_block(state, block):
            total, numer, denom = state
            block_frames, block_places, block_count = block
            patches = jax.vmap(cut)(block_places)
            live = lane < block_count
            grads, numer_b, denom_b = frame_grads(block_frames, patches, probe, forward_table, inverse_table, live)
            total = place_patches(total, grads, block_places)
            return ((total, numer + numer_b, denom + denom_b), None)
        blocks = (frames.reshape(N_POS, FMAX, W, W), places.reshape(N_POS, FMAX, 2), column)
        start = (jnp.zeros((2, OBJ, OBJ), jnp.float32), numer, denom)
        (total, numer, denom), _ = lax.scan(one_block, start, blocks)
        return ((numer, denom), total)
    start = (jnp.zeros((2, W, W), jnp.float32), jnp.zeros((W, W), jnp.float32))
    (numer, denom), object_grad = lax.scan(one_tilt, start, (intensity, positions, counts, object_field))
    return (object_grad, numer / denom[None])
```

```python
import functools

import jax
import jax.numpy as jnp
import numpy as np
from jax import lax
from jax.experimental import pallas as pl
from jax.experimental.pallas import tpu as pltpu
from jax.sharding import PartitionSpec as P

LANES = 128


def dft_tables(length):
    index = np.arange(length, dtype=np.int64)
    phase = (index[:, None] * index[None, :] % length).astype(np.float64) * (
        2.0 * np.pi / length
    )
    cosine = np.cos(phase) / np.sqrt(length)
    sine = np.sin(phase) / np.sqrt(length)
    forward = np.block([[cosine, -sine], [sine, cosine]])
    inverse = np.block([[cosine, sine], [-sine, cosine]])
    return (
        jnp.asarray(forward.astype(np.float32)).astype(jnp.bfloat16),
        jnp.asarray(inverse.astype(np.float32)).astype(jnp.bfloat16),
    )


def frames_kernel(
    reach,
    pos_ref,
    count_ref,
    frames_ref,
    *refs,
):
    blocks = 2 * reach + 1
    block_refs = refs[:blocks]
    probe_ref, fwd_ref, inv_ref = refs[blocks : blocks + 3]
    out_refs = refs[blocks + 3 : 2 * blocks + 3]
    sums_ref = refs[2 * blocks + 3]
    band, total = refs[2 * blocks + 4 :]
    rows = block_refs[0].shape[1]
    groups = block_refs[0].shape[2] // LANES
    width = probe_ref.shape[-1]
    wide = width // LANES

    for b in range(blocks):
        for c in range(2):
            for g in range(groups):
                band[c, g, pl.ds(b * rows, rows), :] = block_refs[b][
                    c, :, g * LANES : (g + 1) * LANES
                ].astype(jnp.float32)
    for c in range(2):
        band[c, groups] = jnp.zeros(band.shape[2:], jnp.float32)
    total[...] = jnp.zeros_like(total)
    sums_ref[...] = jnp.zeros_like(sums_ref)
    first = (lax.axis_index("pos") - reach) * rows

    def one_frame(i, carry):
        r = pos_ref[i, 0] - first
        q = pos_ref[i, 1]
        qb = q // LANES
        qs = q % LANES
        lane = lax.broadcasted_iota(jnp.int32, (width, LANES), 1)
        near = lane < LANES - qs
        back_shift = lax.rem(LANES - qs, LANES)
        patch = []
        for c in range(2):
            rolled = [
                pltpu.roll(band[c, qb + j, pl.ds(r, width), :], back_shift, 1)
                for j in range(wide + 1)
            ]
            patch.append(
                jnp.concatenate(
                    [jnp.where(near, rolled[j], rolled[j + 1]) for j in range(wide)], 1
                )
            )
        pr, pi = probe_ref[0], probe_ref[1]
        xr, xi = patch
        exit_wave = jnp.concatenate(
            [(pr * xr - pi * xi).astype(jnp.bfloat16), (pr * xi + pi * xr).astype(jnp.bfloat16)],
            1,
        )
        half = jnp.dot(exit_wave, fwd_ref[...], preferred_element_type=jnp.float32).astype(
            jnp.bfloat16
        )
        half = jnp.concatenate([half[:, :width], half[:, width:]], 0)
        far = jnp.dot(inv_ref[...], half, preferred_element_type=jnp.float32)
        fr, fi = far[:width], far[width:]
        misfit = fr * fr + fi * fi - frames_ref[i].astype(jnp.float32)
        back = jnp.concatenate(
            [(fr * misfit).astype(jnp.bfloat16), (fi * misfit).astype(jnp.bfloat16)], 0
        )
        mid = jnp.dot(fwd_ref[...], back, preferred_element_type=jnp.float32).astype(jnp.bfloat16)
        mid = jnp.concatenate([mid[:width], mid[width:]], 1)
        wave = jnp.dot(mid, inv_ref[...], preferred_element_type=jnp.float32)
        wr, wi = wave[:, :width], wave[:, width:]
        sums_ref[0] += xr * wr + xi * wi
        sums_ref[1] += xr * wi - xi * wr
        sums_ref[2] += xr * xr + xi * xi
        far_side = lane >= qs
        for c in range(2):
            grad = pr * wr + pi * wi if c == 0 else pr * wi - pi * wr
            grad = grad.astype(jnp.bfloat16).astype(jnp.float32)
            rolled = [
                pltpu.roll(grad[:, j * LANES : (j + 1) * LANES], qs, 1) for j in range(wide)
            ]
            zero = jnp.zeros_like(rolled[0])
            for j in range(wide + 1):
                here = rolled[j] if j < wide else zero
                before = rolled[j - 1] if j > 0 else zero
                total[c, qb + j, pl.ds(r, width), :] += jnp.where(far_side, here, before)
        return carry

    lax.fori_loop(0, count_ref[0, 0], one_frame, 0)
    for b in range(blocks):
        for c in range(2):
            for g in range(groups):
                out_refs[b][c, :, g * LANES : (g + 1) * LANES] = total[
                    c, g, pl.ds(b * rows, rows), :
                ].astype(out_refs[b].dtype)


def frame_sums(reach, positions, count, frames, blocks, probe):
    forward, inverse = dft_tables(probe.shape[-1])
    rows, columns = blocks[0].shape[1:]
    groups = columns // LANES
    n = len(blocks)
    vmem = pl.BlockSpec(memory_space=pltpu.VMEM)
    smem = pl.BlockSpec(memory_space=pltpu.SMEM)
    outs = [
        jax.ShapeDtypeStruct(blocks[0].shape, jnp.float32 if b == reach else jnp.bfloat16)
        for b in range(n)
    ] + [jax.ShapeDtypeStruct((3,) + probe.shape[1:], jnp.float32)]
    return pl.pallas_call(
        functools.partial(frames_kernel, reach),
        out_shape=outs,
        in_specs=[smem, smem, vmem] + [vmem] * (n + 3),
        out_specs=[vmem] * (n + 1),
        scratch_shapes=[
            pltpu.VMEM((2, groups + 1, n * rows, LANES), jnp.float32),
            pltpu.VMEM((2, groups + 1, n * rows, LANES), jnp.float32),
        ],
        compiler_params=pltpu.CompilerParams(vmem_limit_bytes=52 * 1024 * 1024),
    )(positions, count, frames, *blocks, probe, forward, inverse)


def shifted(block, offset, devices):
    pairs = [(p, p + offset) for p in range(devices) if 0 <= p + offset < devices]
    return lax.ppermute(block, "pos", pairs)


def local(devices, intensity, positions, counts, object_field, probe):
    width = probe.shape[-1]
    rows = object_field.shape[2]
    reach = width // rows
    own = object_field[0]
    blocks = [
        own if b == reach else shifted(own, reach - b, devices) for b in range(2 * reach + 1)
    ]
    *grads, sums = frame_sums(reach, positions[0], counts, intensity[0], blocks, probe)
    total = lax.psum(sums, ("tilt", "pos"))
    probe_grad = total[:2] / total[2:]
    object_grad = grads[reach]
    for b in range(2 * reach + 1):
        if b != reach:
            object_grad = object_grad + shifted(grads[b], b - reach, devices).astype(jnp.float32)
    return (object_grad[None], probe_grad)


def solution(mesh):
    placed = (
        P("tilt", "pos", None, None),
        P("tilt", "pos", None),
        P("tilt", "pos"),
        P("tilt", None, "pos", None),
        P(),
    )
    return jax.shard_map(
        functools.partial(local, mesh.shape["pos"]),
        mesh=mesh,
        in_specs=placed,
        out_specs=(P("tilt", None, "pos", None), P()),
        check_vma=False,
    )
```

```python
import functools

import jax
import jax.numpy as jnp
import numpy as np
from jax import lax
from jax.experimental import pallas as pl
from jax.experimental.pallas import tpu as pltpu
from jax.sharding import PartitionSpec as P

LANES = 128


def dft_tables(length):
    index = np.arange(length, dtype=np.int64)
    phase = (index[:, None] * index[None, :] % length).astype(np.float64) * (
        2.0 * np.pi / length
    )
    cosine = np.cos(phase) / np.sqrt(length)
    sine = np.sin(phase) / np.sqrt(length)
    forward = np.block([[cosine, -sine], [sine, cosine]])
    inverse = np.block([[cosine, sine], [-sine, cosine]])
    return (
        jnp.asarray(forward.astype(np.float32)).astype(jnp.bfloat16),
        jnp.asarray(inverse.astype(np.float32)).astype(jnp.bfloat16),
    )


def frames_kernel(
    reach,
    pos_ref,
    count_ref,
    frames_ref,
    *refs,
):
    blocks = 2 * reach + 1
    block_refs = refs[:blocks]
    probe_ref, fwd_ref, inv_ref = refs[blocks : blocks + 3]
    out_refs = refs[blocks + 3 : 2 * blocks + 3]
    sums_ref = refs[2 * blocks + 3]
    chunks_ref = sums_ref
    band, total, sums_ref = refs[2 * blocks + 4 :]
    rows = block_refs[0].shape[1]
    groups = block_refs[0].shape[2] // LANES
    width = probe_ref.shape[-1]
    wide = width // LANES

    for b in range(blocks):
        for c in range(2):
            for g in range(groups):
                band[c, g, pl.ds(b * rows, rows), :] = block_refs[b][
                    c, :, g * LANES : (g + 1) * LANES
                ].astype(jnp.float32)
    for c in range(2):
        band[c, groups] = jnp.zeros(band.shape[2:], jnp.float32)
    total[...] = jnp.zeros_like(total)
    sums_ref[...] = jnp.zeros_like(sums_ref)
    first = (lax.axis_index("pos") - reach) * rows

    def one_frame(i, carry):
        r = pos_ref[i, 0] - first
        q = pos_ref[i, 1]
        qb = q // LANES
        qs = q % LANES
        lane = lax.broadcasted_iota(jnp.int32, (width, LANES), 1)
        near = lane < LANES - qs
        back_shift = lax.rem(LANES - qs, LANES)
        patch = []
        for c in range(2):
            rolled = [
                pltpu.roll(band[c, qb + j, pl.ds(r, width), :], back_shift, 1)
                for j in range(wide + 1)
            ]
            patch.append(
                jnp.concatenate(
                    [jnp.where(near, rolled[j], rolled[j + 1]) for j in range(wide)], 1
                )
            )
        pr, pi = probe_ref[0], probe_ref[1]
        xr, xi = patch
        exit_wave = jnp.concatenate(
            [(pr * xr - pi * xi).astype(jnp.bfloat16), (pr * xi + pi * xr).astype(jnp.bfloat16)],
            1,
        )
        half = jnp.dot(exit_wave, fwd_ref[...], preferred_element_type=jnp.float32).astype(
            jnp.bfloat16
        )
        half = jnp.concatenate([half[:, :width], half[:, width:]], 0)
        far = jnp.dot(inv_ref[...], half, preferred_element_type=jnp.float32)
        fr, fi = far[:width], far[width:]
        misfit = fr * fr + fi * fi - frames_ref[i].astype(jnp.float32)
        back = jnp.concatenate(
            [(fr * misfit).astype(jnp.bfloat16), (fi * misfit).astype(jnp.bfloat16)], 0
        )
        mid = jnp.dot(fwd_ref[...], back, preferred_element_type=jnp.float32).astype(jnp.bfloat16)
        mid = jnp.concatenate([mid[:width], mid[width:]], 1)
        wave = jnp.dot(mid, inv_ref[...], preferred_element_type=jnp.float32)
        wr, wi = wave[:, :width], wave[:, width:]
        sums_ref[0] += xr * wr + xi * wi
        sums_ref[1] += xr * wi - xi * wr
        sums_ref[2] += xr * xr + xi * xi
        far_side = lane >= qs
        for c in range(2):
            grad = pr * wr + pi * wi if c == 0 else pr * wi - pi * wr
            grad = grad.astype(jnp.bfloat16).astype(jnp.float32)
            rolled = [
                pltpu.roll(grad[:, j * LANES : (j + 1) * LANES], qs, 1) for j in range(wide)
            ]
            zero = jnp.zeros_like(rolled[0])
            for j in range(wide + 1):
                here = rolled[j] if j < wide else zero
                before = rolled[j - 1] if j > 0 else zero
                total[c, qb + j, pl.ds(r, width), :] += jnp.where(far_side, here, before)
        return carry

    lax.fori_loop(0, count_ref[0, 0], one_frame, 0)
    for b in range(blocks):
        for c in range(2):
            for g in range(groups):
                out_refs[b][c, :, g * LANES : (g + 1) * LANES] = total[
                    c, g, pl.ds(b * rows, rows), :
                ].astype(out_refs[b].dtype)
    pairs, chips, tilts, _, chunk, _ = chunks_ref.shape
    for e in range(pairs):
        for c in range(chips):
            for t in range(tilts):
                start = ((e * chips + c) * tilts + t) * chunk
                chunks_ref[e, c, t] = sums_ref[:, start : start + chunk, :]


def frame_sums(reach, parts, positions, count, frames, blocks, probe):
    forward, inverse = dft_tables(probe.shape[-1])
    rows, columns = blocks[0].shape[1:]
    groups = columns // LANES
    n = len(blocks)
    vmem = pl.BlockSpec(memory_space=pltpu.VMEM)
    smem = pl.BlockSpec(memory_space=pltpu.SMEM)
    outs = [
        jax.ShapeDtypeStruct(blocks[0].shape, jnp.float32 if b == reach else jnp.bfloat16)
        for b in range(n)
    ] + [jax.ShapeDtypeStruct(parts, jnp.float32)]
    return pl.pallas_call(
        functools.partial(frames_kernel, reach),
        out_shape=outs,
        in_specs=[smem, smem, vmem] + [vmem] * (n + 3),
        out_specs=[vmem] * (n + 1),
        scratch_shapes=[
            pltpu.VMEM((2, groups + 1, n * rows, LANES), jnp.float32),
            pltpu.VMEM((2, groups + 1, n * rows, LANES), jnp.float32),
            pltpu.VMEM((3,) + probe.shape[1:], jnp.float32),
        ],
        compiler_params=pltpu.CompilerParams(vmem_limit_bytes=52 * 1024 * 1024),
    )(positions, count, frames, *blocks, probe, forward, inverse)


def greet(tilts, devices):
    t, p = lax.axis_index("tilt"), lax.axis_index("pos")
    barrier = pltpu.get_barrier_semaphore()
    for k in range(1, devices):
        pl.semaphore_signal(
            barrier,
            inc=1,
            device_id=(t, lax.rem(p + k, devices)),
            device_id_type=pl.DeviceIdType.MESH,
        )
    for k in range(1, tilts):
        pl.semaphore_signal(
            barrier,
            inc=1,
            device_id=(lax.rem(t + k, tilts), p),
            device_id_type=pl.DeviceIdType.MESH,
        )
    pl.semaphore_wait(barrier, devices - 1 + tilts - 1)


def send(src, dst, sem_out, sem_in, tilt, pos):
    return pltpu.make_async_remote_copy(
        src_ref=src,
        dst_ref=dst,
        send_sem=sem_out,
        recv_sem=sem_in,
        device_id=(tilt, pos),
        device_id_type=pl.DeviceIdType.MESH,
    )


def gather_kernel(devices, own_ref, *refs):
    slots = {0: refs[0], 1: refs[1], 3: refs[2], 4: refs[3]}
    out_sem, in_sem = refs[4:]
    t, p = lax.axis_index("tilt"), lax.axis_index("pos")
    chip, chips = p // 2, devices // 2
    greet(1, devices)

    def role(odd):
        partner = p - 1 if odd else p + 1

        def copy(src, slot, out, pos):
            return send(src, slots[slot], out_sem.at[out], in_sem.at[slot], t, pos)

        to_partner = copy(own_ref, 3 if odd else 1, 0, partner)
        to_left = copy(own_ref, 4 if odd else 3, 1, 2 * chip - 1)
        to_right = copy(own_ref, 1 if odd else 0, 2, 2 * chip + 2)
        near, far = (3, 4) if odd else (1, 0)
        forward = copy(slots[near], 4 if odd else 0, 3, partner)
        from_partner = 1 if odd else 3
        opposite = 0 if odd else 4
        has_left, has_right = chip > 0, chip < chips - 1
        outer, inner = (has_right, has_left) if odd else (has_left, has_right)

        def arrived(slot):
            copy(own_ref, slot, 0, partner).wait_recv()

        pl.when(has_left)(to_left.start)
        pl.when(has_right)(to_right.start)
        to_partner.start()

        @pl.when(outer)
        def _():
            arrived(near)
            forward.start()
            arrived(far)
            forward.wait_send()

        arrived(from_partner)
        pl.when(inner)(lambda: arrived(opposite))
        pl.when(has_left)(to_left.wait_send)
        pl.when(has_right)(to_right.wait_send)
        to_partner.wait_send()

    pl.when(lax.rem(p, 2) == 0)(lambda: role(False))
    pl.when(lax.rem(p, 2) == 1)(lambda: role(True))


def gather(devices, own):
    vmem = pl.BlockSpec(memory_space=pltpu.VMEM)
    return pl.pallas_call(
        functools.partial(gather_kernel, devices),
        out_shape=[jax.ShapeDtypeStruct(own.shape, own.dtype)] * 4,
        in_specs=[vmem],
        out_specs=[vmem] * 4,
        scratch_shapes=[pltpu.SemaphoreType.DMA((4,)), pltpu.SemaphoreType.DMA((5,))],
        compiler_params=pltpu.CompilerParams(
            collective_id=1, has_side_effects=True, vmem_limit_bytes=16 * 1024 * 1024
        ),
    )(own)


def exchange_kernel(tilts, devices, *refs):
    grads, sums = refs[:5], refs[5]
    object_ref, probe_ref = refs[6:8]
    mine, extra, from_left, from_right, near = refs[8:13]
    half, plane, column, got0, got1, got2, result = refs[13:20]
    obj_out, obj_in, out0, in0, out1, in1, out2, in2, out3, in3, out4, in4, out5, in5 = refs[20:]
    t, p = lax.axis_index("tilt"), lax.axis_index("pos")
    chip, chips = p // 2, devices // 2
    e = lax.rem(p, 2)
    partner = p + 1 - 2 * e
    greet(tilts, devices)

    swap = send(sums.at[1 - e], got0, out0.at[0], in0.at[0], t, partner)
    swap.start()

    def objects(odd, step):
        has = chip < chips - 1 if odd else chip > 0
        way = 1 if odd else -1
        lands = from_left if odd else from_right
        slot = 2 if odd else 3
        far = send(grads[4 if odd else 0], lands, obj_out.at[2], obj_in.at[slot], t, p + 2 * way)
        close = send(near, lands, obj_out.at[3], obj_in.at[slot], t, p + way)
        to_extra = send(
            grads[0 if odd else 4], extra, obj_out.at[0], obj_in.at[0], t, partner
        )
        to_mine = send(grads[1 if odd else 3], mine, obj_out.at[1], obj_in.at[1], t, partner)
        if step == 0:
            to_extra.start()
            pl.when(has)(far.start)
            to_mine.start()
        elif step == 1:
            to_extra.wait_recv()
            near[...] = (
                grads[3 if odd else 1][...].astype(jnp.float32) + extra[...].astype(jnp.float32)
            ).astype(near.dtype)
            pl.when(has)(close.start)
        else:
            to_mine.wait_recv()
            to_extra.wait_send()
            to_mine.wait_send()

            @pl.when(has)
            def _():
                far.wait_send()
                close.wait_send()

    def both(step):
        pl.when(e == 0)(lambda: objects(False, step))
        pl.when(e == 1)(lambda: objects(True, step))

    both(0)
    swap.wait_recv()
    half[...] = sums[e] + got0[...]
    round1 = []
    for k in range(1, chips):
        other = lax.rem(chip + k, chips)
        round1.append(
            send(half.at[other], got1.at[k - 1], out1.at[k - 1], in1.at[k - 1], t, 2 * other + e)
        )
        round1[-1].start()
    both(1)
    total = half[chip]
    for k in range(1, chips):
        round1[k - 1].wait_recv()
        total = total + got1[k - 1]
    plane[...] = total
    round2 = []
    for k in range(1, tilts):
        other = lax.rem(t + k, tilts)
        round2.append(
            send(plane.at[other], got2.at[k - 1], out2.at[k - 1], in2.at[k - 1], other, p)
        )
        round2[-1].start()
    total = plane[t]
    for k in range(1, tilts):
        round2[k - 1].wait_recv()
        total = total + got2[k - 1]
    column[...] = total[:2] / total[2:]
    result[e, chip, t] = column[...]
    round3 = []
    for k in range(1, tilts):
        other = lax.rem(t + k, tilts)
        round3.append(
            send(column, result.at[e, chip, t], out3.at[k - 1], in3.at[k - 1], other, p)
        )
        round3[-1].start()
    for k in range(1, tilts):
        round3[k - 1].wait_recv()
    round4 = []
    for k in range(1, chips):
        other = lax.rem(chip + k, chips)
        round4.append(
            send(
                result.at[e, chip],
                result.at[e, chip],
                out4.at[k - 1],
                in4.at[k - 1],
                t,
                2 * other + e,
            )
        )
        round4[-1].start()
    for k in range(1, chips):
        round4[k - 1].wait_recv()
    back = send(result.at[e], result.at[e], out5.at[0], in5.at[0], t, partner)
    back.start()

    both(2)
    object_ref[0] = grads[2][...] + mine[...].astype(jnp.float32)

    @pl.when(chip > 0)
    def _():
        send(near, from_left, obj_out.at[3], obj_in.at[2], t, partner).wait_recv()
        object_ref[0] += from_left[...].astype(jnp.float32)

    @pl.when(chip < chips - 1)
    def _():
        send(near, from_right, obj_out.at[3], obj_in.at[3], t, partner).wait_recv()
        object_ref[0] += from_right[...].astype(jnp.float32)

    back.wait_recv()
    chunk = result.shape[-2]
    for i in range(2):
        for c in range(chips):
            for s in range(tilts):
                start = ((i * chips + c) * tilts + s) * chunk
                probe_ref[:, start : start + chunk, :] = result[i, c, s]
    swap.wait_send()
    for copy in round1 + round2 + round3 + round4:
        copy.wait_send()
    back.wait_send()


def exchange(tilts, devices, grads, sums):
    vmem = pl.BlockSpec(memory_space=pltpu.VMEM)
    _, chips, _, planes, chunk, width = sums.shape
    block = grads[0].shape
    dma = pltpu.SemaphoreType.DMA
    f32 = jnp.float32
    return pl.pallas_call(
        functools.partial(exchange_kernel, tilts, devices),
        out_shape=[
            jax.ShapeDtypeStruct((1,) + block, f32),
            jax.ShapeDtypeStruct((2, width, width), f32),
        ],
        in_specs=[vmem] * 6,
        out_specs=[vmem] * 2,
        scratch_shapes=[pltpu.VMEM(block, jnp.bfloat16)] * 5
        + [
            pltpu.VMEM((chips, tilts, planes, chunk, width), f32),
            pltpu.VMEM((tilts, planes, chunk, width), f32),
            pltpu.VMEM((2, chunk, width), f32),
            pltpu.VMEM((chips, tilts, planes, chunk, width), f32),
            pltpu.VMEM((chips - 1, tilts, planes, chunk, width), f32),
            pltpu.VMEM((tilts - 1, planes, chunk, width), f32),
            pltpu.VMEM((2, chips, tilts, 2, chunk, width), f32),
        ]
        + [dma((4,)), dma((4,))]
        + [dma((1,))] * 2
        + [dma((chips - 1,))] * 2
        + [dma((tilts - 1,))] * 4
        + [dma((chips - 1,))] * 2
        + [dma((1,))] * 2,
        compiler_params=pltpu.CompilerParams(
            collective_id=2, has_side_effects=True, vmem_limit_bytes=40 * 1024 * 1024
        ),
    )(*grads, sums)


def local(tilts, devices, intensity, positions, counts, object_field, probe):
    width = probe.shape[-1]
    rows = object_field.shape[2]
    reach = width // rows
    assert reach == 2 and devices % 2 == 0
    own = object_field[0]
    left2, left1, right1, right2 = gather(devices, own)
    blocks = [left2, left1, own, right1, right2]
    parts = (2, devices // 2, tilts, 3, width // (devices * tilts), width)
    *grads, sums = frame_sums(reach, parts, positions[0], counts, intensity[0], blocks, probe)
    return tuple(exchange(tilts, devices, grads, sums))


def solution(mesh):
    placed = (
        P("tilt", "pos", None, None),
        P("tilt", "pos", None),
        P("tilt", "pos"),
        P("tilt", None, "pos", None),
        P(),
    )
    return jax.shard_map(
        functools.partial(local, mesh.shape["tilt"], mesh.shape["pos"]),
        mesh=mesh,
        in_specs=placed,
        out_specs=(P("tilt", None, "pos", None), P()),
        check_vma=False,
    )
```

```python
import functools

import jax
import jax.numpy as jnp
import numpy as np
from jax import lax
from jax.experimental import pallas as pl
from jax.experimental.pallas import tpu as pltpu
from jax.sharding import PartitionSpec as P

LANES = 128


def dft_tables(length):
    index = np.arange(length, dtype=np.int64)
    phase = (index[:, None] * index[None, :] % length).astype(np.float64) * (
        2.0 * np.pi / length
    )
    cosine = np.cos(phase) / np.sqrt(length)
    sine = np.sin(phase) / np.sqrt(length)
    forward = np.block([[cosine, -sine], [sine, cosine]])
    inverse = np.block([[cosine, sine], [-sine, cosine]])
    return (
        jnp.asarray(forward.astype(np.float32)).astype(jnp.bfloat16),
        jnp.asarray(inverse.astype(np.float32)).astype(jnp.bfloat16),
    )


def frames_kernel(
    reach,
    pos_ref,
    count_ref,
    frames_ref,
    *refs,
):
    blocks = 2 * reach + 1
    block_refs = refs[:blocks]
    probe_ref, fwd_ref, inv_ref = refs[blocks : blocks + 3]
    out_refs = refs[blocks + 3 : 2 * blocks + 3]
    sums_ref = refs[2 * blocks + 3]
    chunks_ref = sums_ref
    band, total, sums_ref = refs[2 * blocks + 4 :]
    rows = block_refs[0].shape[1]
    groups = block_refs[0].shape[2] // LANES
    width = probe_ref.shape[-1]
    wide = width // LANES

    for b in range(blocks):
        for c in range(2):
            for g in range(groups):
                band[c, g, pl.ds(b * rows, rows), :] = block_refs[b][
                    c, :, g * LANES : (g + 1) * LANES
                ].astype(jnp.float32)
    for c in range(2):
        band[c, groups] = jnp.zeros(band.shape[2:], jnp.float32)
    total[...] = jnp.zeros_like(total)
    sums_ref[...] = jnp.zeros_like(sums_ref)
    first = (lax.axis_index("pos") - reach) * rows

    lane = lax.broadcasted_iota(jnp.int32, (width, LANES), 1)

    def some_frames(at):
        pr, pi = probe_ref[0], probe_ref[1]
        spots, patches, exits = [], [], []
        for i in at:
            r = pos_ref[0, i] - first
            q = pos_ref[1, i]
            qb, qs = q // LANES, lax.rem(q, LANES)
            spots.append((r, qb, qs))
            near = lane < LANES - qs
            back_shift = lax.rem(LANES - qs, LANES)
            patch = []
            for c in range(2):
                rolled = [
                    pltpu.roll(band[c, qb + j, pl.ds(r, width), :], back_shift, 1)
                    for j in range(wide + 1)
                ]
                patch.append(
                    jnp.concatenate(
                        [jnp.where(near, rolled[j], rolled[j + 1]) for j in range(wide)], 1
                    )
                )
            xr, xi = patch
            patches.append((xr, xi))
            exits.append(
                jnp.concatenate(
                    [
                        (pr * xr - pi * xi).astype(jnp.bfloat16),
                        (pr * xi + pi * xr).astype(jnp.bfloat16),
                    ],
                    1,
                )
            )
        halves = jnp.dot(
            jnp.concatenate(exits, 0), fwd_ref[...], preferred_element_type=jnp.float32
        ).astype(jnp.bfloat16)
        mids = []
        for n, i in enumerate(at):
            half = halves[n * width : (n + 1) * width]
            half = jnp.concatenate([half[:, :width], half[:, width:]], 0)
            far = jnp.dot(inv_ref[...], half, preferred_element_type=jnp.float32)
            fr, fi = far[:width], far[width:]
            misfit = fr * fr + fi * fi - frames_ref[i].astype(jnp.float32)
            back = jnp.concatenate(
                [(fr * misfit).astype(jnp.bfloat16), (fi * misfit).astype(jnp.bfloat16)], 0
            )
            mid = jnp.dot(fwd_ref[...], back, preferred_element_type=jnp.float32).astype(
                jnp.bfloat16
            )
            mids.append(jnp.concatenate([mid[:width], mid[width:]], 1))
        waves = jnp.dot(
            jnp.concatenate(mids, 0), inv_ref[...], preferred_element_type=jnp.float32
        )
        sums = [0.0, 0.0, 0.0]
        for n, i in enumerate(at):
            xr, xi = patches[n]
            wave = waves[n * width : (n + 1) * width]
            wr, wi = wave[:, :width], wave[:, width:]
            sums[0] += xr * wr + xi * wi
            sums[1] += xr * wi - xi * wr
            sums[2] += xr * xr + xi * xi
            r, qb, qs = spots[n]
            far_side = lane >= qs
            for c in range(2):
                grad = pr * wr + pi * wi if c == 0 else pr * wi - pi * wr
                grad = grad.astype(jnp.bfloat16).astype(jnp.float32)
                rolled = [
                    pltpu.roll(grad[:, j * LANES : (j + 1) * LANES], qs, 1)
                    for j in range(wide)
                ]
                zero = jnp.zeros_like(rolled[0])
                for j in range(wide + 1):
                    here = rolled[j] if j < wide else zero
                    before = rolled[j - 1] if j > 0 else zero
                    total[c, qb + j, pl.ds(r, width), :] += jnp.where(far_side, here, before)
        for k in range(3):
            sums_ref[k] += sums[k]

    count = count_ref[0, 0]

    @pl.loop(0, count // 2)
    def _(i):
        some_frames([2 * i, 2 * i + 1])

    @pl.when(lax.rem(count, 2) == 1)
    def _():
        some_frames([count - 1])

    for b in range(blocks):
        for c in range(2):
            for g in range(groups):
                out_refs[b][c, :, g * LANES : (g + 1) * LANES] = total[
                    c, g, pl.ds(b * rows, rows), :
                ].astype(out_refs[b].dtype)
    pairs, chips, tilts, _, chunk, _ = chunks_ref.shape
    for e in range(pairs):
        for c in range(chips):
            for t in range(tilts):
                start = ((e * chips + c) * tilts + t) * chunk
                chunks_ref[e, c, t] = sums_ref[:, start : start + chunk, :]


def frame_sums(reach, parts, positions, count, frames, blocks, probe):
    forward, inverse = dft_tables(probe.shape[-1])
    rows, columns = blocks[0].shape[1:]
    groups = columns // LANES
    n = len(blocks)
    vmem = pl.BlockSpec(memory_space=pltpu.VMEM)
    smem = pl.BlockSpec(memory_space=pltpu.SMEM)
    outs = [
        jax.ShapeDtypeStruct(blocks[0].shape, jnp.float32)
        for b in range(n)
    ] + [jax.ShapeDtypeStruct(parts, jnp.float32)]
    return pl.pallas_call(
        functools.partial(frames_kernel, reach),
        out_shape=outs,
        in_specs=[smem, smem, vmem] + [vmem] * (n + 3),
        out_specs=[vmem] * (n + 1),
        scratch_shapes=[
            pltpu.VMEM((2, groups + 1, n * rows, LANES), jnp.float32),
            pltpu.VMEM((2, groups + 1, n * rows, LANES), jnp.float32),
            pltpu.VMEM((3,) + probe.shape[1:], jnp.float32),
        ],
        compiler_params=pltpu.CompilerParams(vmem_limit_bytes=32 * 1024 * 1024),
    )(positions, count, frames, *blocks, probe, forward, inverse)


def greet(tilts, devices):
    t, p = lax.axis_index("tilt"), lax.axis_index("pos")
    barrier = pltpu.get_barrier_semaphore()
    for k in range(1, devices):
        pl.semaphore_signal(
            barrier,
            inc=1,
            device_id=(t, lax.rem(p + k, devices)),
            device_id_type=pl.DeviceIdType.MESH,
        )
    for k in range(1, tilts):
        pl.semaphore_signal(
            barrier,
            inc=1,
            device_id=(lax.rem(t + k, tilts), p),
            device_id_type=pl.DeviceIdType.MESH,
        )
    pl.semaphore_wait(barrier, devices - 1 + tilts - 1)


def send(src, dst, sem_out, sem_in, tilt, pos):
    return pltpu.make_async_remote_copy(
        src_ref=src,
        dst_ref=dst,
        send_sem=sem_out,
        recv_sem=sem_in,
        device_id=(tilt, pos),
        device_id_type=pl.DeviceIdType.MESH,
    )


def gather_kernel(devices, own_ref, *refs):
    slots = {0: refs[0], 1: refs[1], 3: refs[2], 4: refs[3]}
    out_sem, in_sem = refs[4:]
    t, p = lax.axis_index("tilt"), lax.axis_index("pos")
    chip, chips = p // 2, devices // 2
    greet(1, devices)

    def role(odd):
        partner = p - 1 if odd else p + 1

        def copy(src, slot, out, pos):
            return send(src, slots[slot], out_sem.at[out], in_sem.at[slot], t, pos)

        to_partner = copy(own_ref, 3 if odd else 1, 0, partner)
        to_left = copy(own_ref, 4 if odd else 3, 1, 2 * chip - 1)
        to_right = copy(own_ref, 1 if odd else 0, 2, 2 * chip + 2)
        near, far = (3, 4) if odd else (1, 0)
        forward = copy(slots[near], 4 if odd else 0, 3, partner)
        from_partner = 1 if odd else 3
        opposite = 0 if odd else 4
        has_left, has_right = chip > 0, chip < chips - 1
        outer, inner = (has_right, has_left) if odd else (has_left, has_right)

        def arrived(slot):
            copy(own_ref, slot, 0, partner).wait_recv()

        pl.when(has_left)(to_left.start)
        pl.when(has_right)(to_right.start)
        to_partner.start()

        @pl.when(outer)
        def _():
            arrived(near)
            forward.start()
            arrived(far)
            forward.wait_send()

        arrived(from_partner)
        pl.when(inner)(lambda: arrived(opposite))
        pl.when(has_left)(to_left.wait_send)
        pl.when(has_right)(to_right.wait_send)
        to_partner.wait_send()

    pl.when(lax.rem(p, 2) == 0)(lambda: role(False))
    pl.when(lax.rem(p, 2) == 1)(lambda: role(True))


def gather(devices, own):
    vmem = pl.BlockSpec(memory_space=pltpu.VMEM)
    return pl.pallas_call(
        functools.partial(gather_kernel, devices),
        out_shape=[jax.ShapeDtypeStruct(own.shape, own.dtype)] * 4,
        in_specs=[vmem],
        out_specs=[vmem] * 4,
        scratch_shapes=[pltpu.SemaphoreType.DMA((4,)), pltpu.SemaphoreType.DMA((5,))],
        cost_estimate=pl.CostEstimate(
            flops=0, bytes_accessed=64 * 1024 * 1024, transcendentals=0
        ),
        compiler_params=pltpu.CompilerParams(
            collective_id=1, has_side_effects=True, vmem_limit_bytes=4 * 1024 * 1024
        ),
    )(own)


def exchange_kernel(tilts, devices, *refs):
    grads, sums = refs[:5], refs[5]
    object_ref, probe_ref = refs[6:8]
    mine, extra, from_left, from_right, near, distant = refs[8:14]
    half, plane, column, got0, got1, got2, result = refs[14:21]
    obj_out, obj_in, out0, in0, out1, in1, out2, in2, out3, in3, out4, in4, out5, in5 = refs[21:]
    t, p = lax.axis_index("tilt"), lax.axis_index("pos")
    chip, chips = p // 2, devices // 2
    e = lax.rem(p, 2)
    partner = p + 1 - 2 * e
    greet(tilts, devices)

    swap = send(sums.at[1 - e], got0, out0.at[0], in0.at[0], t, partner)

    def objects(odd, step):
        has = chip < chips - 1 if odd else chip > 0
        way = 1 if odd else -1
        lands = from_left if odd else from_right
        slot = 2 if odd else 3
        far = send(distant, lands, obj_out.at[2], obj_in.at[slot], t, p + 2 * way)
        close = send(near, lands, obj_out.at[3], obj_in.at[slot], t, p + way)
        to_extra = send(
            grads[0 if odd else 4], extra, obj_out.at[0], obj_in.at[0], t, partner
        )
        to_mine = send(grads[1 if odd else 3], mine, obj_out.at[1], obj_in.at[1], t, partner)
        if step == 0:
            to_extra.start()
            swap.start()
            distant[...] = grads[4 if odd else 0][...].astype(distant.dtype)
            pl.when(has)(far.start)
            to_mine.start()
        elif step == 1:
            to_extra.wait_recv()
            near[...] = (
                grads[3 if odd else 1][...] + extra[...]
            ).astype(near.dtype)
            pl.when(has)(close.start)
        else:
            to_mine.wait_recv()
            to_extra.wait_send()
            to_mine.wait_send()

            @pl.when(has)
            def _():
                far.wait_send()
                close.wait_send()

    def both(step):
        pl.when(e == 0)(lambda: objects(False, step))
        pl.when(e == 1)(lambda: objects(True, step))

    both(0)
    swap.wait_recv()
    half[...] = sums[e] + got0[...]
    round1 = []
    for k in range(1, chips):
        other = lax.rem(chip + k, chips)
        round1.append(
            send(half.at[other], got1.at[k - 1], out1.at[k - 1], in1.at[k - 1], t, 2 * other + e)
        )
        round1[-1].start()
    both(1)
    total = half[chip]
    for k in range(1, chips):
        round1[k - 1].wait_recv()
        total = total + got1[k - 1]
    plane[...] = total
    round2 = []
    for k in range(1, tilts):
        other = lax.rem(t + k, tilts)
        round2.append(
            send(plane.at[other], got2.at[k - 1], out2.at[k - 1], in2.at[k - 1], other, p)
        )
        round2[-1].start()
    total = plane[t]
    for k in range(1, tilts):
        round2[k - 1].wait_recv()
        total = total + got2[k - 1]
    column[...] = total[:2] / total[2:]
    result[e, chip, t] = column[...]
    round3 = []
    for k in range(1, tilts):
        other = lax.rem(t + k, tilts)
        round3.append(
            send(column, result.at[e, chip, t], out3.at[k - 1], in3.at[k - 1], other, p)
        )
        round3[-1].start()
    for k in range(1, tilts):
        round3[k - 1].wait_recv()
    round4 = []
    for k in range(1, chips):
        other = lax.rem(chip + k, chips)
        round4.append(
            send(
                result.at[e, chip],
                result.at[e, chip],
                out4.at[k - 1],
                in4.at[k - 1],
                t,
                2 * other + e,
            )
        )
        round4[-1].start()
    for k in range(1, chips):
        round4[k - 1].wait_recv()
    back = send(result.at[e], result.at[e], out5.at[0], in5.at[0], t, partner)
    back.start()

    both(2)
    object_ref[0] = grads[2][...] + mine[...]

    @pl.when(chip > 0)
    def _():
        send(near, from_left, obj_out.at[3], obj_in.at[2], t, partner).wait_recv()
        object_ref[0] += from_left[...].astype(jnp.float32)

    @pl.when(chip < chips - 1)
    def _():
        send(near, from_right, obj_out.at[3], obj_in.at[3], t, partner).wait_recv()
        object_ref[0] += from_right[...].astype(jnp.float32)

    back.wait_recv()
    chunk = result.shape[-2]
    for i in range(2):
        for c in range(chips):
            for s in range(tilts):
                start = ((i * chips + c) * tilts + s) * chunk
                probe_ref[:, start : start + chunk, :] = result[i, c, s]
    swap.wait_send()
    for copy in round1 + round2 + round3 + round4:
        copy.wait_send()
    back.wait_send()


def exchange(tilts, devices, grads, sums):
    vmem = pl.BlockSpec(memory_space=pltpu.VMEM)
    _, chips, _, planes, chunk, width = sums.shape
    block = grads[0].shape
    dma = pltpu.SemaphoreType.DMA
    f32 = jnp.float32
    return pl.pallas_call(
        functools.partial(exchange_kernel, tilts, devices),
        out_shape=[
            jax.ShapeDtypeStruct((1,) + block, f32),
            jax.ShapeDtypeStruct((2, width, width), f32),
        ],
        in_specs=[vmem] * 6,
        out_specs=[vmem] * 2,
        scratch_shapes=[pltpu.VMEM(block, f32)] * 2
        + [pltpu.VMEM(block, jnp.bfloat16)] * 4
        + [
            pltpu.VMEM((chips, tilts, planes, chunk, width), f32),
            pltpu.VMEM((tilts, planes, chunk, width), f32),
            pltpu.VMEM((2, chunk, width), f32),
            pltpu.VMEM((chips, tilts, planes, chunk, width), f32),
            pltpu.VMEM((chips - 1, tilts, planes, chunk, width), f32),
            pltpu.VMEM((tilts - 1, planes, chunk, width), f32),
            pltpu.VMEM((2, chips, tilts, 2, chunk, width), f32),
        ]
        + [dma((4,)), dma((4,))]
        + [dma((1,))] * 2
        + [dma((chips - 1,))] * 2
        + [dma((tilts - 1,))] * 4
        + [dma((chips - 1,))] * 2
        + [dma((1,))] * 2,
        compiler_params=pltpu.CompilerParams(
            collective_id=2, has_side_effects=True, vmem_limit_bytes=20 * 1024 * 1024
        ),
    )(*grads, sums)


def local(tilts, devices, intensity, positions, counts, object_field, probe):
    width = probe.shape[-1]
    rows = object_field.shape[2]
    reach = width // rows
    assert reach == 2 and devices % 2 == 0
    own = object_field[0]
    left2, left1, right1, right2 = gather(devices, own)
    blocks = [left2, left1, own, right1, right2]
    parts = (2, devices // 2, tilts, 3, width // (devices * tilts), width)
    *grads, sums = frame_sums(reach, parts, positions[0].T, counts, intensity[0], blocks, probe)
    return tuple(exchange(tilts, devices, grads, sums))


def solution(mesh):
    placed = (
        P("tilt", "pos", None, None),
        P("tilt", "pos", None),
        P("tilt", "pos"),
        P("tilt", None, "pos", None),
        P(),
    )
    return jax.shard_map(
        functools.partial(local, mesh.shape["tilt"], mesh.shape["pos"]),
        mesh=mesh,
        in_specs=placed,
        out_specs=(P("tilt", None, "pos", None), P()),
        check_vma=False,
    )
```
